32 devices in a mesh: groups: 2 (over y), batch: 4 (over x, core), mp: 4 (over z).
Axes of the slice: x: 2, y: 2, z: 4, core: 2. Of those that a mesh axis runs over, the one named last changes fastest.
Arguments:
- tokens: bfloat16 [512, 8192], P(('groups', 'batch')), parts along dimension 0, may hold values from -6 to 6
- gate_weight: bfloat16 [8192, 26624], P('batch', 'mp'), may hold values from -0.0625 to 0.0625
- up_weight: bfloat16 [8192, 26624], P('batch', 'mp'), may hold values from -0.0625 to 0.0625
- down_weight: bfloat16 [26624, 8192], P('mp', 'batch'), may hold values from -0.0390625 to 0.0390625
Outputs:
- mixed: bfloat16 [512, 8192], P(('groups', 'mp'), 'batch'), parts along dimension 0
The draws below stay inside these ranges and needn't reach their ends.
There are 2 independent parts, one for each index of `groups`. The reference program is written for one: setup_inputs(seed, part) draws one part's arguments, and reference() takes and returns one part's arrays. A program takes and returns all parts, laid end to end along the dimension named above; an argument that names none is the same for every part. Nothing has to cross between parts.
All inputs are finite; a program needn't handle non-finite values.
Results may differ from the reference program's by a relative error of at most 0.017.
Values may be sent and summed in bfloat16 or wider, within the bound.
A program may use at most 192 MiB of HBM per device.

```python
import jax
import jax.numpy as jnp
from jax import lax

D = 8192
FF = 26624
TOKENS = 256
N_BATCH = 4
N_MP = 4


def block_levels(rng, dims, cuts, smallest, top_value):
    def one(axis_at, blocks):
        draws = jax.random.uniform(jax.random.fold_in(jax.random.fold_in(rng, 6), axis_at), (blocks,), jnp.float32, smallest / len(cuts), top_value / len(cuts))
        return jnp.repeat(jnp.exp(draws), dims[axis_at] // blocks).reshape((-1,) + (1,) * (len(dims) - axis_at - 1))

    gain = one(*cuts[0])
    for cut in cuts[1:]:
        gain = gain * one(*cut)
    return gain


def noise(own_key, shape, deviation, most, split=(), dtype=jnp.bfloat16):
    values = jax.random.normal(own_key, shape, jnp.float32) * deviation
    if len(split) > 0:
        values = block_levels(own_key, shape, split, -0.22, 0.18) * values
    return jnp.clip(values, min=-most, max=most).astype(dtype)


def setup_inputs(seed: int = 0, part: int = 0) -> dict:
    key_of = jax.random.split(jax.random.key(seed), 5)
    part_keys = jax.random.split(jax.random.fold_in(key_of[4], part), 5)
    return {
        "tokens": noise(part_keys[0], (TOKENS, D), 1.0, 6.0, ((0, 4),)),
        "gate_weight": noise(key_of[1], (D, FF), D ** -0.5, 0.0625, ((0, 4), (1, 4))),
        "up_weight": noise(key_of[2], (D, FF), D ** -0.5, 0.0625, ((0, 4), (1, 4))),
        "down_weight": noise(key_of[3], (FF, D), FF ** -0.5, 0.0390625, ((0, 4), (1, 4))),
    }


def reference(tokens, gate_weight, up_weight, down_weight):
    width_block = D // N_BATCH
    token_blocks = tokens.reshape(TOKENS, N_BATCH, width_block).transpose(1, 0, 2)
    gate_blocks = gate_weight.reshape(N_BATCH, width_block, FF)
    up_blocks = up_weight.reshape(N_BATCH, width_block, FF)

    def add_part(totals, triple):
        block_tokens, block_gate, block_up = triple
        gate_part = jnp.dot(block_tokens, block_gate, preferred_element_type=jnp.float32).astype(jnp.bfloat16)
        up_part = jnp.dot(block_tokens, block_up, preferred_element_type=jnp.float32).astype(jnp.bfloat16)
        gate_part, up_part = lax.optimization_barrier((gate_part, up_part))
        return (totals[0] + gate_part.astype(jnp.float32), totals[1] + up_part.astype(jnp.float32)), None

    start = (jnp.zeros((TOKENS, FF), jnp.float32), jnp.zeros((TOKENS, FF), jnp.float32))
    sums, unused = lax.scan(add_part, start, (token_blocks, gate_blocks, up_blocks))
    hidden = (jax.nn.silu(sums[0]) * sums[1]).astype(jnp.bfloat16)
    ff_block = FF // N_MP
    hidden_blocks = hidden.reshape(TOKENS, N_MP, ff_block).transpose(1, 0, 2)
    down_blocks = down_weight.reshape(N_MP, ff_block, D)

    def add_term(total, pair):
        block_hidden, block_down = pair
        term = jnp.dot(block_hidden, block_down, preferred_element_type=jnp.float32).astype(jnp.bfloat16)
        term = lax.optimization_barrier(term)
        return total + term.astype(jnp.float32), None

    total, unused_two = lax.scan(add_term, jnp.zeros((TOKENS, D), jnp.float32), (hidden_blocks, down_blocks))
    return (tokens.astype(jnp.float32) + total).astype(jnp.bfloat16)
```

```python
import functools

import jax
import jax.numpy as jnp
from jax import lax
from jax.experimental import pallas as pl
from jax.experimental.pallas import tpu as pltpu
from jax.sharding import PartitionSpec as P

MESH = pl.DeviceIdType.MESH
SLOTS = 3
LAG_C, LAG_D, LAG_E = 3, 4, 5


def kernel(
    mp, chunks, tokens, gate_w, up_w, down_w, out,
    acts, gate_s, up_s, down_s, away, kept, from_core, from_x, hid, total, line_out, line_in,
    own_sem, gate_sem, up_sem, down_sem, tok_send, tok_recv,
    core_send, core_recv, x_send, x_recv, hx_send, hx_recv, hc_send, hc_recv, hf_send, hf_recv,
    line_send, line_recv,
):
    f32, bf16 = jnp.float32, jnp.bfloat16
    me, z = lax.axis_index("batch"), lax.axis_index("mp")
    x, c = lax.div(me, 2), lax.rem(me, 2)
    sibling, across, diagonal = x * 2 + 1 - c, (1 - x) * 2 + c, (1 - x) * 2 + 1 - c
    rows, depth = tokens.shape[0], acts.shape[1]
    width = hid.shape[2]
    tile = min(256, width)

    def block(r):
        return pl.ds(r * rows, rows)

    def weights(i, ref, slots, sem, axis):
        window = pl.ds(pl.multiple_of(i * width, width), width)
        src = ref.at[:, window] if axis else ref.at[window, :]
        slot = lax.rem(i, SLOTS)
        return pltpu.make_async_copy(src, slots.at[slot], sem.at[slot])

    def gate_up(i):
        return weights(i, gate_w, gate_s, gate_sem, 1), weights(i, up_w, up_s, up_sem, 1)

    def down(i):
        return weights(i, down_w, down_s, down_sem, 0)

    def remote(src, dst, send, recv, **place):
        return pltpu.make_async_remote_copy(
            src_ref=src, dst_ref=dst, send_sem=send, recv_sem=recv, device_id=place, device_id_type=MESH
        )

    def columns(index):
        return pl.ds(pl.multiple_of(index * depth, depth), depth)

    own_copy = pltpu.make_async_copy(tokens.at[:, columns(me)], acts.at[block(0), :], own_sem)
    own_copy.start()
    for i in range(SLOTS):
        for copy in gate_up(i):
            copy.start()
    for i in range(SLOTS):
        down(i).start()

    barrier = pltpu.get_barrier_semaphore()
    for peer in (sibling, across, diagonal):
        pl.semaphore_signal(barrier, inc=1, device_id={"batch": peer}, device_id_type=MESH)

    @pl.when(z > 0)
    def _():
        pl.semaphore_signal(barrier, inc=1, device_id={"mp": z - 1}, device_id_type=MESH)

    @pl.when(z < mp - 1)
    def _():
        pl.semaphore_signal(barrier, inc=1, device_id={"mp": z + 1}, device_id_type=MESH)

    @pl.when((z > 0) & (z < mp - 1))
    def _():
        pl.semaphore_wait(barrier, 5)

    @pl.when((z == 0) | (z == mp - 1))
    def _():
        pl.semaphore_wait(barrier, 4)

    token_copies = [
        remote(tokens.at[:, columns(peer)], acts.at[block(r), :], tok_send.at[r], tok_recv.at[r], batch=peer)
        for r, peer in ((1, across), (3, diagonal), (2, sibling))
    ]
    for copy in token_copies:
        copy.start()
    total[...] = jnp.zeros_like(total)
    own_copy.wait()
    for copy in token_copies:
        copy.wait_recv()

    def core_copy(j):
        return remote(away.at[j], from_core.at[j], core_send.at[j], core_recv.at[j], batch=sibling)

    def x_copy(j):
        return remote(kept.at[j, block(1), :], from_x.at[j], x_send.at[j], x_recv.at[j], batch=across)

    def hid_x(j):
        return remote(hid.at[j, block(0), :], hid.at[j, block(1), :], hx_send.at[j], hx_recv.at[j], batch=across)

    def hid_core(j):
        return remote(hid.at[j, block(0), :], hid.at[j, block(2), :], hc_send.at[j], hc_recv.at[j], batch=sibling)

    def hid_forward(j):
        return remote(hid.at[j, block(1), :], hid.at[j, block(3), :], hf_send.at[j], hf_recv.at[j], batch=sibling)

    def step(i, carry):
        @pl.when(i < chunks)
        def _():
            for copy in gate_up(i):
                copy.wait()
            slot = lax.rem(i, SLOTS)
            for part, ref in enumerate((gate_s, up_s)):
                for n in range(width // tile):
                    product = jnp.dot(
                        acts[...], ref[slot, :, n * tile:(n + 1) * tile], preferred_element_type=f32
                    ).astype(bf16)
                    at = part * width + n * tile
                    kept[i, :, at:at + tile] = product[:2 * rows]
                    away[i, :, at:at + tile] = product[2 * rows:]
            core_copy(i).start()

            @pl.when(i + SLOTS < chunks)
            def _():
                for copy in gate_up(i + SLOTS):
                    copy.start()

        @pl.when((i >= 1) & (i < chunks + 1))
        def _():
            j = i - 1
            core_copy(j).wait_recv()
            kept[j, block(1), :] = (
                kept[j, block(1), :].astype(f32) + from_core[j, block(1), :].astype(f32)
            ).astype(bf16)
            x_copy(j).start()

        @pl.when((i >= LAG_C) & (i < chunks + LAG_C))
        def _():
            j = i - LAG_C
            x_copy(j).wait_recv()
            summed = (
                kept[j, block(0), :].astype(f32) + from_core[j, block(0), :].astype(f32) + from_x[j].astype(f32)
            )
            gate, up = summed[:, :width], summed[:, width:]
            hid[j, block(0), :] = (gate / (1.0 + jnp.exp(-gate)) * up).astype(bf16)
            hid_x(j).start()
            hid_core(j).start()

        @pl.when((i >= LAG_D) & (i < chunks + LAG_D))
        def _():
            j = i - LAG_D
            hid_x(j).wait_recv()
            hid_forward(j).start()

        @pl.when(i >= LAG_E)
        def _():
            j = i - LAG_E
            slot = lax.rem(j, SLOTS)
            down(j).wait()
            hid_core(j).wait_recv()
            hid_forward(j).wait_recv()
            for n in range(depth // tile):
                at = pl.ds(n * tile, tile)
                total[:, at] += jnp.dot(hid[j], down_s[slot, :, at], preferred_element_type=f32)

            @pl.when(j + SLOTS < chunks)
            def _():
                down(j + SLOTS).start()

        return carry

    lax.fori_loop(0, chunks + LAG_E, step, 0)

    def place(m):
        dx, dc = lax.rem(lax.div(m, 2) + x, 2), lax.rem(lax.rem(m, 2) + c, 2)
        return pl.ds(pl.multiple_of((dc * 2 + dx) * rows, rows), rows)

    def line_copy(way, m, to):
        return remote(line_out.at[way, m], line_in.at[way, m], line_send.at[way, m], line_recv.at[way, m], mp=to)

    def flow(way, m, sends, first, to):
        @pl.when(sends)
        def _():
            line_out[way, m] = total[place(m), :].astype(bf16)

            @pl.when(jnp.logical_not(first))
            def _():
                line_copy(way, m, to).wait_recv()
                line_out[way, m] = (total[place(m), :] + line_in[way, m].astype(f32)).astype(bf16)

            line_copy(way, m, to).start()

    for k in range(mp - 1):
        flow(0, mp - 1 - k, z < mp - 1 - k, z == 0, lax.rem(z + 1, mp))
        flow(1, k, z > k, z == mp - 1, lax.rem(z + mp - 1, mp))

    total[place(z), :] = total[place(z), :] + acts[place(z), :].astype(f32)

    @pl.when(z > 0)
    def _():
        line_copy(0, z, lax.rem(z + 1, mp)).wait_recv()
        total[place(z), :] = total[place(z), :] + line_in[0, z].astype(f32)

    @pl.when(z < mp - 1)
    def _():
        line_copy(1, z, lax.rem(z + 1, mp)).wait_recv()
        total[place(z), :] = total[place(z), :] + line_in[1, z].astype(f32)

    out[...] = total[place(z), :].astype(bf16)

    for copy in token_copies:
        copy.wait_send()

    def drain(j, carry):
        for copy in (core_copy, x_copy, hid_x, hid_core, hid_forward):
            copy(j).wait_send()
        return carry

    lax.fori_loop(0, chunks, drain, 0)
    for k in range(mp - 1):
        @pl.when(z < mp - 1 - k)
        def _():
            line_copy(0, mp - 1 - k, lax.rem(z + 1, mp)).wait_send()

        @pl.when(z > k)
        def _():
            line_copy(1, k, lax.rem(z + mp - 1, mp)).wait_send()


def fused(mp, chunks, tokens, gate_weight, up_weight, down_weight):
    rows = tokens.shape[0]
    depth, hidden = gate_weight.shape
    width = hidden // chunks
    bf16, dma = jnp.bfloat16, pltpu.SemaphoreType.DMA
    return pl.pallas_call(
        functools.partial(kernel, mp, chunks),
        out_shape=jax.ShapeDtypeStruct((rows, depth), bf16),
        in_specs=[pl.BlockSpec(memory_space=pl.ANY)] * 4,
        out_specs=pl.BlockSpec(memory_space=pltpu.VMEM),
        scratch_shapes=[
            pltpu.VMEM((4 * rows, depth), bf16),
            pltpu.VMEM((SLOTS, depth, width), bf16),
            pltpu.VMEM((SLOTS, depth, width), bf16),
            pltpu.VMEM((SLOTS, width, depth), bf16),
            pltpu.VMEM((chunks, 2 * rows, 2 * width), bf16),
            pltpu.VMEM((chunks, 2 * rows, 2 * width), bf16),
            pltpu.VMEM((chunks, 2 * rows, 2 * width), bf16),
            pltpu.VMEM((chunks, rows, 2 * width), bf16),
            pltpu.VMEM((chunks, 4 * rows, width), bf16),
            pltpu.VMEM((4 * rows, depth), jnp.float32),
            pltpu.VMEM((2, mp, rows, depth), bf16),
            pltpu.VMEM((2, mp, rows, depth), bf16),
            dma(()),
            dma((SLOTS,)), dma((SLOTS,)), dma((SLOTS,)),
            dma((4,)), dma((4,)),
        ] + [dma((chunks,))] * 10 + [dma((2, mp)), dma((2, mp))],
        compiler_params=pltpu.CompilerParams(
            collective_id=0, has_side_effects=True, vmem_limit_bytes=56 * 2**20
        ),
        cost_estimate=pl.CostEstimate(
            flops=4 * rows * depth * hidden * 6, bytes_accessed=6 * depth * hidden, transcendentals=rows * hidden
        ),
    )(tokens, gate_weight, up_weight, down_weight)


def plain(tokens, gate_weight, up_weight, down_weight):
    hidden_width = gate_weight.shape[1]
    exchanged = lax.all_to_all(tokens, "batch", split_axis=1, concat_axis=0, tiled=True)
    both_weights = jnp.concatenate([gate_weight, up_weight], axis=1)
    summed = lax.psum_scatter(
        jnp.dot(exchanged, both_weights, preferred_element_type=jnp.float32).astype(jnp.bfloat16),
        "batch",
        scatter_dimension=0,
        tiled=True,
    ).astype(jnp.float32)
    hidden = (jax.nn.silu(summed[:, :hidden_width]) * summed[:, hidden_width:]).astype(jnp.bfloat16)
    terms = jnp.dot(
        lax.all_gather(hidden, "batch", axis=0, tiled=True),
        down_weight,
        preferred_element_type=jnp.float32,
    )
    shared = lax.psum_scatter(
        terms.astype(jnp.bfloat16), "mp", scatter_dimension=0, tiled=True
    ).astype(jnp.float32)
    row_count = shared.shape[0]
    own_part = lax.dynamic_slice_in_dim(exchanged, lax.axis_index("mp") * row_count, row_count, 0)
    return (own_part.astype(jnp.float32) + shared).astype(jnp.bfloat16)


def solution(mesh):
    placed = (P(("groups", "batch"), None), P("batch", "mp"), P("batch", "mp"), P("mp", "batch"))
    batch, mp = mesh.shape["batch"], mesh.shape["mp"]
    local = functools.partial(fused, mp, 13) if batch == 4 and mp == 4 else plain
    return jax.shard_map(
        local, mesh=mesh, in_specs=placed, out_specs=P(("groups", "mp"), "batch"), check_vma=False
    )
```

```python
import functools

import jax
import jax.numpy as jnp
from jax import lax
from jax.experimental import pallas as pl
from jax.experimental.pallas import tpu as pltpu
from jax.sharding import PartitionSpec as P

MESH = pl.DeviceIdType.MESH
SLOTS = 3
LAG_C, LAG_D, LAG_E = 2, 3, 4


def kernel(
    mp, chunks, tokens, gate_w, up_w, down_w, out,
    acts, gate_s, up_s, down_s, away, kept, from_core, from_x, hid, total, term_out, term_in,
    own_sem, gate_sem, up_sem, down_sem, tok_send, tok_recv,
    core_send, core_recv, x_send, x_recv, hx_send, hx_recv, hc_send, hc_recv, hf_send, hf_recv,
    term_send, term_recv,
):
    f32, bf16 = jnp.float32, jnp.bfloat16
    me, z = lax.axis_index("batch"), lax.axis_index("mp")
    x, c = lax.div(me, 2), lax.rem(me, 2)
    sibling, across, diagonal = x * 2 + 1 - c, (1 - x) * 2 + c, (1 - x) * 2 + 1 - c
    rows, depth = tokens.shape[0], acts.shape[1]
    width = hid.shape[2]
    tile = min(256, width)

    def block(r):
        return pl.ds(r * rows, rows)

    def weights(i, ref, slots, sem, axis):
        window = pl.ds(pl.multiple_of(i * width, width), width)
        src = ref.at[:, window] if axis else ref.at[window, :]
        slot = lax.rem(i, SLOTS)
        return pltpu.make_async_copy(src, slots.at[slot], sem.at[slot])

    def gate_up(i):
        return weights(i, gate_w, gate_s, gate_sem, 1), weights(i, up_w, up_s, up_sem, 1)

    def down(i):
        return weights(i, down_w, down_s, down_sem, 0)

    def remote(src, dst, send, recv, **place):
        return pltpu.make_async_remote_copy(
            src_ref=src, dst_ref=dst, send_sem=send, recv_sem=recv, device_id=place, device_id_type=MESH
        )

    def columns(index):
        return pl.ds(pl.multiple_of(index * depth, depth), depth)

    own_copy = pltpu.make_async_copy(tokens.at[:, columns(me)], acts.at[block(0), :], own_sem)
    own_copy.start()
    for i in range(SLOTS):
        for copy in gate_up(i):
            copy.start()
    for i in range(SLOTS):
        down(i).start()

    barrier = pltpu.get_barrier_semaphore()
    for peer in (sibling, across, diagonal):
        pl.semaphore_signal(barrier, inc=1, device_id={"batch": peer}, device_id_type=MESH)

    for d in range(1, mp):
        pl.semaphore_signal(barrier, inc=1, device_id={"mp": lax.rem(z + d, mp)}, device_id_type=MESH)
    pl.semaphore_wait(barrier, 3 + mp - 1)

    token_copies = [
        remote(tokens.at[:, columns(peer)], acts.at[block(r), :], tok_send.at[r], tok_recv.at[r], batch=peer)
        for r, peer in ((1, across), (3, diagonal), (2, sibling))
    ]
    for copy in token_copies:
        copy.start()
    total[...] = jnp.zeros_like(total)
    own_copy.wait()
    for copy in token_copies:
        copy.wait_recv()

    def core_copy(j):
        return remote(away.at[j], from_core.at[j], core_send.at[j], core_recv.at[j], batch=sibling)

    def x_copy(j):
        return remote(kept.at[j, block(1), :], from_x.at[j], x_send.at[j], x_recv.at[j], batch=across)

    def hid_x(j):
        return remote(hid.at[j, block(0), :], hid.at[j, block(1), :], hx_send.at[j], hx_recv.at[j], batch=across)

    def hid_core(j):
        return remote(hid.at[j, block(0), :], hid.at[j, block(2), :], hc_send.at[j], hc_recv.at[j], batch=sibling)

    def hid_forward(j):
        return remote(hid.at[j, block(1), :], hid.at[j, block(3), :], hf_send.at[j], hf_recv.at[j], batch=sibling)

    def step(i, carry):
        @pl.when(i < chunks)
        def _():
            for copy in gate_up(i):
                copy.wait()
            slot = lax.rem(i, SLOTS)
            for part, ref in enumerate((gate_s, up_s)):
                for n in range(width // tile):
                    product = jnp.dot(
                        acts[...], ref[slot, :, n * tile:(n + 1) * tile], preferred_element_type=f32
                    ).astype(bf16)
                    at = part * width + n * tile
                    kept[i, :, at:at + tile] = product[:2 * rows]
                    away[i, :, at:at + tile] = product[2 * rows:]
            core_copy(i).start()

            @pl.when(i + SLOTS < chunks)
            def _():
                for copy in gate_up(i + SLOTS):
                    copy.start()

        @pl.when((i >= 1) & (i < chunks + 1))
        def _():
            j = i - 1
            core_copy(j).wait_recv()
            kept[j, block(1), :] = (
                kept[j, block(1), :].astype(f32) + from_core[j, block(1), :].astype(f32)
            ).astype(bf16)
            x_copy(j).start()

        @pl.when((i >= LAG_C) & (i < chunks + LAG_C))
        def _():
            j = i - LAG_C
            x_copy(j).wait_recv()
            summed = (
                kept[j, block(0), :].astype(f32) + from_core[j, block(0), :].astype(f32) + from_x[j].astype(f32)
            )
            gate, up = summed[:, :width], summed[:, width:]
            hid[j, block(0), :] = (gate / (1.0 + jnp.exp(-gate)) * up).astype(bf16)
            hid_x(j).start()
            hid_core(j).start()

        @pl.when((i >= LAG_D) & (i < chunks + LAG_D))
        def _():
            j = i - LAG_D
            hid_x(j).wait_recv()
            hid_forward(j).start()

        @pl.when(i >= LAG_E)
        def _():
            j = i - LAG_E
            slot = lax.rem(j, SLOTS)
            down(j).wait()
            hid_core(j).wait_recv()
            hid_forward(j).wait_recv()
            for n in range(depth // tile):
                at = pl.ds(n * tile, tile)
                total[:, at] += jnp.dot(hid[j], down_s[slot, :, at], preferred_element_type=f32)

            @pl.when(j + SLOTS < chunks)
            def _():
                down(j + SLOTS).start()

        return carry

    lax.fori_loop(0, chunks + LAG_E, step, 0)

    def place(m):
        dx, dc = lax.rem(lax.div(m, 2) + x, 2), lax.rem(lax.rem(m, 2) + c, 2)
        return pl.ds(pl.multiple_of((dc * 2 + dx) * rows, rows), rows)

    def term_copy(d):
        return remote(
            term_out.at[d - 1], term_in.at[d - 1], term_send.at[d - 1], term_recv.at[d - 1], mp=lax.rem(z + d, mp)
        )

    for d in range(1, mp):
        term_out[d - 1] = total[place(lax.rem(z + d, mp)), :].astype(bf16)
        term_copy(d).start()
    mine = total[place(z), :] + acts[place(z), :].astype(f32)
    for d in range(1, mp):
        term_copy(d).wait_recv()
        mine = mine + term_in[d - 1].astype(f32)
    out[...] = mine.astype(bf16)

    for copy in token_copies:
        copy.wait_send()

    def drain(j, carry):
        for copy in (core_copy, x_copy, hid_x, hid_core, hid_forward):
            copy(j).wait_send()
        return carry

    lax.fori_loop(0, chunks, drain, 0)
    for d in range(1, mp):
        term_copy(d).wait_send()


def fused(mp, chunks, tokens, gate_weight, up_weight, down_weight):
    rows = tokens.shape[0]
    depth, hidden = gate_weight.shape
    width = hidden // chunks
    bf16, dma = jnp.bfloat16, pltpu.SemaphoreType.DMA
    return pl.pallas_call(
        functools.partial(kernel, mp, chunks),
        out_shape=jax.ShapeDtypeStruct((rows, depth), bf16),
        in_specs=[pl.BlockSpec(memory_space=pl.ANY)] * 4,
        out_specs=pl.BlockSpec(memory_space=pltpu.VMEM),
        scratch_shapes=[
            pltpu.VMEM((4 * rows, depth), bf16),
            pltpu.VMEM((SLOTS, depth, width), bf16),
            pltpu.VMEM((SLOTS, depth, width), bf16),
            pltpu.VMEM((SLOTS, width, depth), bf16),
            pltpu.VMEM((chunks, 2 * rows, 2 * width), bf16),
            pltpu.VMEM((chunks, 2 * rows, 2 * width), bf16),
            pltpu.VMEM((chunks, 2 * rows, 2 * width), bf16),
            pltpu.VMEM((chunks, rows, 2 * width), bf16),
            pltpu.VMEM((chunks, 4 * rows, width), bf16),
            pltpu.VMEM((4 * rows, depth), jnp.float32),
            pltpu.VMEM((mp - 1, rows, depth), bf16),
            pltpu.VMEM((mp - 1, rows, depth), bf16),
            dma(()),
            dma((SLOTS,)), dma((SLOTS,)), dma((SLOTS,)),
            dma((4,)), dma((4,)),
        ] + [dma((chunks,))] * 10 + [dma((mp - 1,)), dma((mp - 1,))],
        compiler_params=pltpu.CompilerParams(
            collective_id=0, has_side_effects=True, vmem_limit_bytes=56 * 2**20
        ),
        cost_estimate=pl.CostEstimate(
            flops=4 * rows * depth * hidden * 6, bytes_accessed=6 * depth * hidden, transcendentals=rows * hidden
        ),
    )(tokens, gate_weight, up_weight, down_weight)


def plain(tokens, gate_weight, up_weight, down_weight):
    hidden_width = gate_weight.shape[1]
    exchanged = lax.all_to_all(tokens, "batch", split_axis=1, concat_axis=0, tiled=True)
    both_weights = jnp.concatenate([gate_weight, up_weight], axis=1)
    summed = lax.psum_scatter(
        jnp.dot(exchanged, both_weights, preferred_element_type=jnp.float32).astype(jnp.bfloat16),
        "batch",
        scatter_dimension=0,
        tiled=True,
    ).astype(jnp.float32)
    hidden = (jax.nn.silu(summed[:, :hidden_width]) * summed[:, hidden_width:]).astype(jnp.bfloat16)
    terms = jnp.dot(
        lax.all_gather(hidden, "batch", axis=0, tiled=True),
        down_weight,
        preferred_element_type=jnp.float32,
    )
    shared = lax.psum_scatter(
        terms.astype(jnp.bfloat16), "mp", scatter_dimension=0, tiled=True
    ).astype(jnp.float32)
    row_count = shared.shape[0]
    own_part = lax.dynamic_slice_in_dim(exchanged, lax.axis_index("mp") * row_count, row_count, 0)
    return (own_part.astype(jnp.float32) + shared).astype(jnp.bfloat16)


def solution(mesh):
    placed = (P(("groups", "batch"), None), P("batch", "mp"), P("batch", "mp"), P("mp", "batch"))
    batch, mp = mesh.shape["batch"], mesh.shape["mp"]
    local = functools.partial(fused, mp, 13) if batch == 4 and mp == 4 else plain
    return jax.shard_map(
        local, mesh=mesh, in_specs=placed, out_specs=P(("groups", "mp"), "batch"), check_vma=False
    )
```
